32 devices in a mesh: parts: 2 (over x), slab: 8 (over z, y), vblk: 2 (over core).
Axes of the slice: x: 2, y: 2, z: 4, core: 2. Of those that a mesh axis runs over, the one named last changes fastest.
Arguments:
- vectors: float32 [2, 3, 160, 12288], P(None, None, 'vblk', ('parts', 'slab')), parts along dimension 3, may hold values from -6 to 6
- links: float32 [2, 3, 9, 12288], P(None, None, None, ('parts', 'slab')), parts along dimension 3, may hold values from -4 to 4
- rotation: float32 [2, 160, 160], replicated, may hold values from -0.3125 to 0.3125
Outputs:
- rotated: float32 [2, 3, 160, 12288], P(None, None, 'vblk', ('parts', 'slab')), parts along dimension 3
- gram: float32 [4, 160, 160], P('parts', None, 'vblk'), parts along dimension 0
- projected: float32 [4, 160, 160], P('parts', None, 'vblk'), parts along dimension 0
The draws below stay inside these ranges and needn't reach their ends.
There are 2 independent parts, one for each index of `parts`. The reference program is written for one: setup_inputs(seed, part) draws one part's arguments, and reference() takes and returns one part's arrays. A program takes and returns all parts, laid end to end along the dimension named above; an argument that names none is the same for every part. Nothing has to cross between parts.
All inputs are finite; a program needn't handle non-finite values.
Results may differ from the reference program's by a relative error of at most 0.000071.
Values sent between devices are 32-bit elements; how exact they have to be, the bound alone decides.
A program may use at most 192 MiB of HBM per device.

```python
import jax
import jax.numpy as jnp
from jax import lax

NV = 160
LX = 96
LY = 4
LZ = 2
GY = 4
GZ = 2
SITES = 6144
NY = 16
NZ = 4


def steps_of(rng, dims, pieces, least, high):
    gain, own = 1.0, jax.random.fold_in(rng, 6)
    for dim, parts in pieces:
        draws = jnp.exp(jax.random.uniform(jax.random.fold_in(own, dim), (parts,), jnp.float32, least / len(pieces), high / len(pieces)))
        gain = gain * jnp.repeat(draws, dims[dim] // parts).reshape([-1 if axis == dim else 1 for axis in range(len(dims))])
    return gain


def scatter_about(stream_key, extent, width, most, cuts=(), dtype=jnp.bfloat16):
    level = steps_of(stream_key, extent, cuts, -0.22, 0.18) if cuts else 1.0
    values = jax.random.normal(stream_key, extent, jnp.float32) * width * level
    return jnp.minimum(jnp.maximum(values, -most), most).astype(dtype)


def setup_inputs(seed: int = 0, part: int = 0) -> dict:
    key_of = jax.random.split(jax.random.key(seed), 4)
    part_splits = jax.random.split(jax.random.fold_in(key_of[3], part), 4)
    return {
        "vectors": scatter_about(part_splits[0], (2, 3, NV, SITES), 1.0, 6.0, ((2, 2), (3, 8)), jnp.float32),
        "links": scatter_about(part_splits[1], (2, 3, 9, SITES), 0.3, 4.0, ((3, 8),), jnp.float32),
        "rotation": scatter_about(key_of[2], (2, NV, NV), (2 * NV) ** -0.5, 0.3125, (), jnp.float32),
    }


center_shift = 8.0
half_width = 6.0


def contract(matrix, operand):
    return jnp.sum(matrix[:, :, None] * operand[None], axis=1)


def link_times(link, field):
    real_part = contract(link[0], field[0]) - contract(link[1], field[1])
    imag_part = contract(link[0], field[1]) + contract(link[1], field[0])
    return jnp.stack([real_part, imag_part], axis=0)


def adjoint_times(link, field):
    link_real = jnp.swapaxes(link[0], 0, 1)
    link_imag = jnp.swapaxes(link[1], 0, 1)
    real_part = contract(link_real, field[0]) + contract(link_imag, field[1])
    imag_part = contract(link_real, field[1]) - contract(link_imag, field[0])
    return jnp.stack([real_part, imag_part], axis=0)


def apply_step(padded, links_pad):
    center = padded[:, :, :, 1:-1, 1:-1]
    link_x = links_pad[:, :, 0:3, 1:-1, 1:-1]
    hopped = link_times(link_x, jnp.roll(center, -1, axis=5))
    hopped = hopped + adjoint_times(jnp.roll(link_x, 1, axis=5), jnp.roll(center, 1, axis=5))
    link_y = links_pad[:, :, 3:6]
    hopped = hopped + link_times(link_y[:, :, :, 1:-1, 1:-1], padded[:, :, :, 1:-1, 2:])
    hopped = hopped + adjoint_times(link_y[:, :, :, 1:-1, :-2], padded[:, :, :, 1:-1, :-2])
    link_z = links_pad[:, :, 6:9]
    hopped = hopped + link_times(link_z[:, :, :, 1:-1, 1:-1], padded[:, :, :, 2:, 1:-1])
    hopped = hopped + adjoint_times(link_z[:, :, :, :-2, 1:-1], padded[:, :, :, :-2, 1:-1])
    return ((6.0 - center_shift) * center - hopped) / half_width


def to_grid(field):
    lead = field.shape[:3]
    folded = field.reshape(lead + (GZ, GY, LZ, LY, LX))
    folded = jnp.transpose(folded, (0, 1, 2, 3, 5, 4, 6, 7))
    return folded.reshape(lead + (NZ, NY, LX))


def to_blocks(grid):
    lead = grid.shape[:3]
    folded = grid.reshape(lead + (GZ, LZ, GY, LY, LX))
    folded = jnp.transpose(folded, (0, 1, 2, 3, 5, 4, 6, 7))
    return folded.reshape(lead + (SITES,))


def zero_pad(field):
    return jnp.pad(field, ((0, 0), (0, 0), (0, 0), (1, 1), (1, 1), (0, 0)))


def site_inner(left_arr, right_arr):
    return jnp.einsum("cvs,cws->vw", left_arr, right_arr, precision=lax.Precision.HIGHEST)


def hermitian(left_arr, right_arr):
    real_part = site_inner(left_arr[0], right_arr[0]) + site_inner(left_arr[1], right_arr[1])
    imag_part = site_inner(left_arr[0], right_arr[1]) - site_inner(left_arr[1], right_arr[0])
    return jnp.stack([real_part, imag_part], axis=0)


def vector_mix(field, matrix):
    return jnp.einsum("cvs,vw->cws", field, matrix, precision=lax.Precision.HIGHEST)


def rotate(field, matrix):
    real_part = vector_mix(field[0], matrix[0]) - vector_mix(field[1], matrix[1])
    imag_part = vector_mix(field[0], matrix[1]) + vector_mix(field[1], matrix[0])
    return jnp.stack([real_part, imag_part], axis=0)


def reference(vectors, links, rotation):
    block_size = 16 if NV % 16 == 0 else NV
    blocks_count = NV // block_size
    links_pad = zero_pad(to_grid(links))

    def filter_block(block_vecs):
        first = apply_step(zero_pad(block_vecs), links_pad)
        filtered = 2.0 * apply_step(zero_pad(first), links_pad) - block_vecs
        image_field = apply_step(zero_pad(filtered), links_pad)
        return filtered, image_field

    grid_vecs = to_grid(vectors)
    grouped = grid_vecs.reshape(2, 3, blocks_count, block_size, NZ, NY, LX)
    grouped = jnp.moveaxis(grouped, 2, 0)
    filtered, image_field = lax.map(filter_block, grouped)
    filtered = jnp.moveaxis(filtered, 0, 2).reshape(2, 3, NV, NZ, NY, LX)
    image_field = jnp.moveaxis(image_field, 0, 2).reshape(2, 3, NV, NZ, NY, LX)
    filtered = to_blocks(filtered)
    image_field = to_blocks(image_field)
    site_total = 3.0 * SITES
    gram = hermitian(filtered, filtered) / site_total
    projected = hermitian(filtered, image_field) / site_total
    rotated = rotate(filtered, rotation)
    return rotated, gram, projected
```

```python
import functools

import jax
import jax.numpy as jnp
from jax import lax
from jax.experimental import pallas as pl
from jax.experimental.pallas import tpu as pltpu
from jax.sharding import PartitionSpec as P

LX = 96
LY = 4
LZ = 2
GY = 4
LAYER = LY * LX
CHUNK = 16
MESH = pl.DeviceIdType.MESH

center_shift = 8.0
half_width = 6.0
OWN = 6.0 - center_shift


def edge_mask(shape, x):
    lane = lax.broadcasted_iota(jnp.int32, shape, 1)
    mask = lane == x
    for row in range(1, LY):
        mask = mask | (lane == row * LX + x)
    return mask


def x_forward(layer):
    return jnp.where(
        edge_mask(layer.shape, LX - 1),
        pltpu.roll(layer, LX - 1, 1),
        pltpu.roll(layer, LAYER - 1, 1),
    )


def x_backward(layer):
    return jnp.where(
        edge_mask(layer.shape, 0),
        pltpu.roll(layer, LAYER - LX + 1, 1),
        pltpu.roll(layer, 1, 1),
    )


def y_forward(layer, after):
    joined = jnp.concatenate([layer, after], axis=1)
    return pltpu.roll(joined, LAYER + 128 - LX, 1)[:, :LAYER]


def y_backward(layer, before):
    joined = jnp.concatenate([before, layer], axis=1)
    return pltpu.roll(joined, LAYER + LX, 1)[:, :LAYER]


def halves(x):
    high = x.astype(jnp.bfloat16)
    low = (x - high.astype(jnp.float32)).astype(jnp.bfloat16)
    return high, low


def split_dot(left, right, dims):
    dot = functools.partial(
        lax.dot_general, dimension_numbers=(dims, ((), ())), preferred_element_type=jnp.float32
    )
    return dot(left[0], right[0]) + (dot(left[0], right[1]) + dot(left[1], right[0]))


def kernel(
    n, rows, vec_ref, link_ref, turn_ref, out_ref, gram_ref, proj_ref,
    e_v, e_first, e_filt, y_before, y_after, link_y, link_z, spread, moved,
    f_other, b_own, b_other, sums, part, slots, total,
    in_sem, halo_send, halo_recv, link_send, link_recv, pair_send, pair_recv,
    part_send, part_recv, total_send, total_recv,
):
    me = lax.axis_index("slab")
    core = lax.axis_index("vblk")
    count = vec_ref.shape[2]
    chunks = count // CHUNK
    row_pos = lax.rem(me, GY)
    has_up = me + GY < n
    has_down = me >= GY
    has_next = row_pos < GY - 1
    has_prev = row_pos > 0
    fields = (e_v, e_first, e_filt)

    loads = [
        pltpu.make_async_copy(
            vec_ref.at[:, :, :, pl.ds(z * LAYER, LAYER)], e_v.at[:, :, 1 + z], in_sem.at[z]
        )
        for z in range(LZ)
    ]
    for load in loads:
        load.start()

    barrier = pltpu.get_barrier_semaphore()
    pl.semaphore_signal(barrier, inc=1, device_id={"vblk": 1 - core}, device_id_type=MESH)

    def greet(d, carry):
        pl.semaphore_signal(
            barrier, inc=1, device_id={"slab": lax.rem(me + d, n)}, device_id_type=MESH
        )
        return carry

    lax.fori_loop(1, n, greet, 0)

    @pl.when(jnp.logical_not(has_down))
    def _():
        link_z[...] = jnp.zeros_like(link_z)
        for field in fields:
            field[:, :, 0] = jnp.zeros(field.shape[:2] + field.shape[3:], jnp.float32)

    @pl.when(jnp.logical_not(has_up))
    def _():
        for field in fields:
            field[:, :, LZ + 1] = jnp.zeros(field.shape[:2] + field.shape[3:], jnp.float32)

    @pl.when(jnp.logical_not(has_prev))
    def _():
        link_y[...] = jnp.zeros_like(link_y)
        y_before[...] = jnp.zeros_like(y_before)

    @pl.when(jnp.logical_not(has_next))
    def _():
        y_after[...] = jnp.zeros_like(y_after)

    for load in loads:
        load.wait()
    pl.semaphore_wait(barrier, n)

    def halo(stage, kind, chunk):
        field = fields[stage]
        own = pl.ds(pl.multiple_of(chunk * CHUNK, CHUNK), CHUNK)
        src, dst, to = (
            (field.at[:, :, LZ, own], field.at[:, :, 0, own], me + GY),
            (field.at[:, :, 1, own], field.at[:, :, LZ + 1, own], me - GY),
            (
                field.at[:, :, pl.ds(1, LZ), own, pl.ds(0, 128)],
                y_after.at[stage, :, :, :, own],
                me - 1,
            ),
            (
                field.at[:, :, pl.ds(1, LZ), own, pl.ds(LAYER - 128, 128)],
                y_before.at[min(stage, 1), :, :, :, own],
                me + 1,
            ),
        )[kind]
        return pltpu.make_async_remote_copy(
            src_ref=src, dst_ref=dst,
            send_sem=halo_send.at[stage, kind, chunk],
            recv_sem=halo_recv.at[stage, kind, chunk],
            device_id={"slab": to}, device_id_type=MESH,
        )

    sends = (has_up, has_down, has_prev, has_next)
    receives = (has_down, has_up, has_next, has_prev)
    kinds = ((0, 1, 2, 3), (0, 1, 2, 3), (1, 2))

    def start_halo(stage, chunk):
        for kind in kinds[stage]:
            pl.when(sends[kind])(lambda kind=kind: halo(stage, kind, chunk).start())

    def await_halo(stage, chunk):
        for kind in kinds[stage]:
            pl.when(receives[kind])(lambda kind=kind: halo(stage, kind, chunk).wait_recv())

    def link_copy(index):
        if index < LZ:
            src = link_ref.at[1, :, pl.ds((index + 1) * LAYER - 128, 128)]
            dst, to = link_y.at[index], me + 1
        else:
            src = link_ref.at[2, :, pl.ds((LZ - 1) * LAYER, LAYER)]
            dst, to = link_z, me + GY
        return pltpu.make_async_remote_copy(
            src_ref=src, dst_ref=dst, send_sem=link_send.at[index],
            recv_sem=link_recv.at[index], device_id={"slab": to}, device_id_type=MESH,
        )

    def pair_copy(which, chunk):
        own = pl.ds(pl.multiple_of(chunk * CHUNK, CHUNK), CHUNK)
        src = e_filt.at[:, :, pl.ds(1, LZ), own] if which == 0 else b_own.at[:, :, :, own]
        dst = (f_other, b_other)[which].at[:, :, :, own]
        return pltpu.make_async_remote_copy(
            src_ref=src, dst_ref=dst, send_sem=pair_send.at[which, chunk],
            recv_sem=pair_recv.at[which, chunk],
            device_id={"vblk": 1 - core}, device_id_type=MESH,
        )

    def loop(body):
        def step(chunk, carry):
            body(chunk)
            return carry

        lax.fori_loop(0, chunks, step, 0)

    @pl.when(has_next)
    def _():
        for index in range(LZ):
            link_copy(index).start()

    @pl.when(has_up)
    def _():
        link_copy(LZ).start()

    loop(lambda chunk: start_halo(0, chunk))

    @pl.when(has_prev)
    def _():
        for index in range(LZ):
            link_copy(index).wait_recv()

    @pl.when(has_down)
    def _():
        link_copy(LZ).wait_recv()

    for z in range(LZ):
        lanes = pl.ds(z * LAYER, LAYER)
        forward = [link_ref[mu, :, lanes] for mu in range(3)]
        below = link_z[...] if z == 0 else link_ref[2, :, pl.ds((z - 1) * LAYER, LAYER)]
        backward = [x_backward(forward[0]), y_backward(forward[1], link_y[z]), below]
        for side, table in enumerate((forward, backward)):
            for mu in range(3):
                for k in range(18):
                    spread[side, mu, k, z] = jnp.broadcast_to(
                        table[mu][k : k + 1], (8, LAYER)
                    )

    def hop(stage, chunk, finish):
        field = fields[stage]
        both = stage < 2
        own = pl.ds(pl.multiple_of(chunk * CHUNK, CHUNK), CHUNK)

        def shift(z, carry):
            for part_id in range(2):
                for colour in range(3):
                    layer = field[part_id, colour, z + 1, own, :]
                    moved[0, part_id, colour, z] = x_forward(layer)
                    moved[1, part_id, colour, z] = y_forward(
                        layer, y_after[stage, part_id, colour, z, own, :]
                    )
                    if both:
                        moved[2, part_id, colour, z] = x_backward(layer)
                        moved[3, part_id, colour, z] = y_backward(
                            layer, y_before[stage, part_id, colour, z, own, :]
                        )
            return carry

        lax.fori_loop(0, LZ, shift, 0)

        def tile(index, carry):
            z = index // (LAYER // 128)
            lanes = pl.ds(pl.multiple_of(lax.rem(index, LAYER // 128) * 128, 128), 128)

            def take(ref, *at):
                return ref[at].reshape(CHUNK // 8, 8, 128)

            acc_re = [None] * 3
            acc_im = [None] * 3
            for mu in range(3):
                for side in range(2 if both else 1):
                    if mu == 2:
                        here = [
                            take(field, c // 3, c % 3, z + (0 if side else 2), own, lanes)
                            for c in range(6)
                        ]
                    else:
                        here = [
                            take(moved, 2 * side + mu, c // 3, c % 3, z, slice(None), lanes)
                            for c in range(6)
                        ]
                    for row in range(3):
                        for col in range(3):
                            k = row * 3 + col if side == 0 else col * 3 + row
                            link_re = spread[side, mu, k, z, :, lanes]
                            link_im = spread[side, mu, 9 + k, z, :, lanes]
                            re, im = here[col], here[3 + col]
                            if side == 0:
                                real = link_re * re - link_im * im
                                imag = link_re * im + link_im * re
                            else:
                                real = link_re * re + link_im * im
                                imag = link_re * im - link_im * re
                            if acc_re[row] is None:
                                acc_re[row], acc_im[row] = real, imag
                            else:
                                acc_re[row] = acc_re[row] + real
                                acc_im[row] = acc_im[row] + imag
            for row in range(3):
                for part_id, value in ((0, acc_re[row]), (1, acc_im[row])):
                    finish(part_id, row, z, own, lanes, value)
            return carry

        lax.fori_loop(0, LZ * LAYER // 128, tile, 0)

    def merged(ref, part_id, row, z, own, lanes):
        return ref[part_id, row, z, own, lanes].reshape(CHUNK // 8, 8, 128)

    def finish_first(part_id, row, z, own, lanes, value):
        center = merged(e_v, part_id, row, z + 1, own, lanes)
        done = (OWN * center - value) * (1.0 / half_width)
        e_first[part_id, row, z + 1, own, lanes] = done.reshape(CHUNK, 128)

    def finish_filtered(part_id, row, z, own, lanes, value):
        center = merged(e_first, part_id, row, z + 1, own, lanes)
        start = merged(e_v, part_id, row, z + 1, own, lanes)
        done = (OWN * center - value) * (2.0 / half_width) - start
        e_filt[part_id, row, z + 1, own, lanes] = done.reshape(CHUNK, 128)

    def finish_bonds(part_id, row, z, own, lanes, value):
        b_own[part_id, row, z, own, lanes] = value.reshape(CHUNK, 128)

    def do_first(chunk):
        await_halo(0, chunk)
        hop(0, chunk, finish_first)
        start_halo(1, chunk)

    def do_filtered(chunk):
        await_halo(1, chunk)
        hop(1, chunk, finish_filtered)
        pair_copy(0, chunk).start()
        start_halo(2, chunk)

    def do_bonds(chunk):
        await_halo(2, chunk)
        hop(2, chunk, finish_bonds)
        pair_copy(1, chunk).start()

    loop(do_first)
    loop(do_filtered)
    loop(lambda chunk: pair_copy(0, chunk).wait_recv())

    def stacked(ref, colour, z):
        return halves(jnp.concatenate([ref[0, colour, z], ref[1, colour, z]], axis=0))

    lane_dims = ((1,), (1,))
    sums[...] = jnp.zeros_like(sums)
    turn = [halves(turn_ref[side]) for side in range(2)]

    for colour in range(3):
        for z in range(LZ):
            mine = stacked(e_filt, colour, z + 1)
            other = stacked(f_other, colour, z)
            sums[0] += split_dot(mine, mine, lane_dims)
            sums[1] += split_dot(other, mine, lane_dims)
            turned = split_dot(turn[0], mine, ((1,), (0,)))
            turned = turned + split_dot(turn[1], other, ((1,), (0,)))
            for part_id in range(2):
                out_ref[part_id, colour, :, pl.ds(z * LAYER, LAYER)] = turned[
                    part_id * count : (part_id + 1) * count
                ]

    loop(do_bonds)
    loop(lambda chunk: pair_copy(1, chunk).wait_recv())

    for colour in range(3):
        for z in range(LZ):
            mine = stacked(e_filt, colour, z + 1)
            other = stacked(f_other, colour, z)
            bond = stacked(b_own, colour, z)
            bond_other = stacked(b_other, colour, z)
            sums[2] += split_dot(mine, bond, lane_dims) + split_dot(bond, mine, lane_dims)
            sums[3] += split_dot(other, bond, lane_dims) + split_dot(bond_other, mine, lane_dims)

    def inner(index):
        top = sums[index, pl.ds(0, count), :]
        low = sums[index, pl.ds(count, count), :]
        return (
            top[:, :count] + low[:, count:],
            top[:, count:] - low[:, :count],
        )

    sites = 3.0 * n * vec_ref.shape[3]
    fill = jnp.zeros((count, 128 - count), jnp.float32)
    for side, at in ((0, core), (1, 1 - core)):
        gram = inner(side)
        hopped = inner(2 + side)
        for part_id in range(2):
            projected = (OWN * gram[part_id] - hopped[part_id]) * (1.0 / half_width)
            for base, value in ((0, gram[part_id]), (2, projected)):
                first_row = pl.multiple_of((base + part_id) * 2 * count + at * count, 8)
                part[pl.ds(first_row, count), :] = jnp.concatenate(
                    [value * (1.0 / sites), fill], axis=1
                )

    owners = part.shape[0] // rows

    def rows_of(owner):
        return pl.ds(pl.multiple_of(owner * rows, 8), rows)

    def part_copy(d):
        owner = lax.rem(me + d, n)
        return owner, pltpu.make_async_remote_copy(
            src_ref=part.at[rows_of(jnp.minimum(owner, owners - 1))],
            dst_ref=slots.at[d], send_sem=part_send.at[d], recv_sem=part_recv.at[d],
            device_id={"slab": owner}, device_id_type=MESH,
        )

    def total_copy(d):
        source = jnp.minimum(me, owners - 1)
        return pltpu.make_async_remote_copy(
            src_ref=total.at[rows_of(source)], dst_ref=total.at[rows_of(source)],
            send_sem=total_send.at[d], recv_sem=total_recv.at[d],
            device_id={"slab": lax.rem(me + d, n)}, device_id_type=MESH,
        )

    def total_arrival(d):
        source = lax.rem(me + n - d, n)
        where = rows_of(jnp.minimum(source, owners - 1))
        return source, pltpu.make_async_remote_copy(
            src_ref=total.at[where], dst_ref=total.at[where],
            send_sem=total_send.at[d], recv_sem=total_recv.at[d],
            device_id={"slab": lax.rem(me + d, n)}, device_id_type=MESH,
        )

    def around(body):
        def step(d, carry):
            body(d)
            return carry

        lax.fori_loop(1, n, step, 0)

    def send_part(d):
        owner, copy = part_copy(d)
        pl.when(owner < owners)(copy.start)

    def end_part(d):
        owner, copy = part_copy(d)
        pl.when(owner < owners)(copy.wait_send)

    around(send_part)

    @pl.when(me < owners)
    def _():
        mine = rows_of(jnp.minimum(me, owners - 1))
        around(lambda d: part_copy(d)[1].wait_recv())
        total[mine, :] = lax.fori_loop(
            1, n, lambda d, running: running + slots[d], part[mine, :]
        )
        around(lambda d: total_copy(d).start())

    def end_total(d):
        source, copy = total_arrival(d)
        pl.when(source < owners)(copy.wait_recv)

    around(end_total)
    for ref, base in ((gram_ref, 0), (proj_ref, 2)):
        for part_id in range(2):
            ref[part_id] = total[
                pl.ds((base + part_id) * 2 * count, 2 * count), pl.ds(0, count)
            ]

    def end_sends(chunk):
        for stage in range(3):
            for kind in kinds[stage]:
                pl.when(sends[kind])(
                    lambda stage=stage, kind=kind: halo(stage, kind, chunk).wait_send()
                )
        for which in range(2):
            pair_copy(which, chunk).wait_send()

    loop(end_sends)

    @pl.when(has_next)
    def _():
        for index in range(LZ):
            link_copy(index).wait_send()

    @pl.when(has_up)
    def _():
        link_copy(LZ).wait_send()

    around(end_part)

    @pl.when(me < owners)
    def _():
        around(lambda d: total_copy(d).wait_send())


def per_device(n, vectors, links, rotation):
    count, local_sites = vectors.shape[2], vectors.shape[3]
    core = lax.axis_index("vblk")
    link_rows = links.reshape(2, 3, 3, 3, local_sites)
    link_rows = jnp.transpose(link_rows, (2, 0, 1, 3, 4)).reshape(3, 18, local_sites)
    columns = lax.dynamic_slice_in_dim(rotation, core * count, count, 2)
    columns = jnp.swapaxes(columns, 1, 2)
    blocks = []
    for side in (core, 1 - core):
        own = lax.dynamic_slice_in_dim(columns, side * count, count, 2)
        top = jnp.concatenate([own[0], -own[1]], axis=1)
        low = jnp.concatenate([own[1], own[0]], axis=1)
        blocks.append(jnp.concatenate([top, low], axis=0))
    turn = jnp.stack(blocks)

    chunks = count // CHUNK
    all_rows = 4 * 2 * count
    rows = -(-all_rows // n)
    while all_rows % rows or rows % 8:
        rows += 1
    f32 = jnp.float32
    halo_shape = (2, 3, LZ + 2, count, LAYER)
    block = (2, 3, LZ, count, LAYER)
    vmem = pl.BlockSpec(memory_space=pltpu.VMEM)
    return pl.pallas_call(
        functools.partial(kernel, n, rows),
        out_shape=(
            jax.ShapeDtypeStruct(vectors.shape, f32),
            jax.ShapeDtypeStruct((2, 2 * count, count), f32),
            jax.ShapeDtypeStruct((2, 2 * count, count), f32),
        ),
        in_specs=[pl.BlockSpec(memory_space=pl.ANY), vmem, vmem],
        out_specs=(vmem, vmem, vmem),
        scratch_shapes=[
            pltpu.VMEM(halo_shape, f32),
            pltpu.VMEM(halo_shape, f32),
            pltpu.VMEM(halo_shape, f32),
            pltpu.VMEM((2, 2, 3, LZ, count, 128), f32),
            pltpu.VMEM((3, 2, 3, LZ, count, 128), f32),
            pltpu.VMEM((LZ, 18, 128), f32),
            pltpu.VMEM((18, LAYER), f32),
            pltpu.VMEM((2, 3, 18, LZ, 8, LAYER), f32),
            pltpu.VMEM((4, 2, 3, LZ, CHUNK, LAYER), f32),
            pltpu.VMEM(block, f32),
            pltpu.VMEM(block, f32),
            pltpu.VMEM(block, f32),
            pltpu.VMEM((4, 2 * count, 2 * count), f32),
            pltpu.VMEM((all_rows, 128), f32),
            pltpu.VMEM((n, rows, 128), f32),
            pltpu.VMEM((all_rows, 128), f32),
            pltpu.SemaphoreType.DMA((LZ,)),
            pltpu.SemaphoreType.DMA((3, 4, chunks)),
            pltpu.SemaphoreType.DMA((3, 4, chunks)),
            pltpu.SemaphoreType.DMA((LZ + 1,)),
            pltpu.SemaphoreType.DMA((LZ + 1,)),
            pltpu.SemaphoreType.DMA((2, chunks)),
            pltpu.SemaphoreType.DMA((2, chunks)),
            pltpu.SemaphoreType.DMA((n,)),
            pltpu.SemaphoreType.DMA((n,)),
            pltpu.SemaphoreType.DMA((n,)),
            pltpu.SemaphoreType.DMA((n,)),
        ],
        compiler_params=pltpu.CompilerParams(
            collective_id=0, has_side_effects=True, vmem_limit_bytes=56 * 1024 * 1024
        ),
    )(vectors, link_rows, turn)


def solution(mesh):
    in_specs = (
        P(None, None, "vblk", ("parts", "slab")),
        P(None, None, None, ("parts", "slab")),
        P(),
    )
    out_specs = (
        P(None, None, "vblk", ("parts", "slab")),
        P("parts", None, "vblk"),
        P("parts", None, "vblk"),
    )
    return jax.shard_map(
        functools.partial(per_device, mesh.shape["slab"]),
        mesh=mesh, in_specs=in_specs, out_specs=out_specs, check_vma=False,
    )
```

```python
import functools

import jax
import jax.numpy as jnp
from jax import lax
from jax.experimental import pallas as pl
from jax.experimental.pallas import tpu as pltpu
from jax.sharding import PartitionSpec as P

LX = 96
LY = 4
LZ = 2
GY = 4
LAYER = LY * LX
CHUNK = 16
MESH = pl.DeviceIdType.MESH

center_shift = 8.0
half_width = 6.0
OWN = 6.0 - center_shift


def edge_mask(shape, x):
    lane = lax.broadcasted_iota(jnp.int32, shape, 1)
    mask = lane == x
    for row in range(1, LY):
        mask = mask | (lane == row * LX + x)
    return mask


def x_forward(layer):
    return jnp.where(
        edge_mask(layer.shape, LX - 1),
        pltpu.roll(layer, LX - 1, 1),
        pltpu.roll(layer, LAYER - 1, 1),
    )


def x_backward(layer):
    return jnp.where(
        edge_mask(layer.shape, 0),
        pltpu.roll(layer, LAYER - LX + 1, 1),
        pltpu.roll(layer, 1, 1),
    )


def y_forward(layer, after):
    joined = jnp.concatenate([layer, after], axis=1)
    return pltpu.roll(joined, LAYER + 128 - LX, 1)[:, :LAYER]


def y_backward(layer, before):
    joined = jnp.concatenate([before, layer], axis=1)
    return pltpu.roll(joined, LAYER + LX, 1)[:, :LAYER]


def halves(x):
    high = x.astype(jnp.bfloat16)
    low = (x - high.astype(jnp.float32)).astype(jnp.bfloat16)
    return high, low


def split_dot(left, right, dims):
    dot = functools.partial(
        lax.dot_general, dimension_numbers=(dims, ((), ())), preferred_element_type=jnp.float32
    )
    return dot(left[0], right[0]) + (dot(left[0], right[1]) + dot(left[1], right[0]))


def kernel(
    n, rows, vec_ref, link_ref, turn_ref, out_ref, gram_ref, proj_ref,
    e_v, e_first, e_filt, y_before, y_after, link_y, link_z, spread, moved,
    f_other, b_own, b_other, sums, part, slots, total,
    in_sem, halo_send, halo_recv, link_send, link_recv, pair_send, pair_recv,
    part_send, part_recv, total_send, total_recv,
):
    me = lax.axis_index("slab")
    core = lax.axis_index("vblk")
    count = vec_ref.shape[2]
    chunks = count // CHUNK
    row_pos = lax.rem(me, GY)
    has_up = me + GY < n
    has_down = me >= GY
    has_next = row_pos < GY - 1
    has_prev = row_pos > 0
    fields = (e_v, e_first, e_filt)
    low_rows = row_pos < GY // 2
    high_rows = jnp.logical_not(low_rows)

    loads = [
        pltpu.make_async_copy(
            vec_ref.at[:, :, :, pl.ds(z * LAYER, LAYER)], e_v.at[:, :, 1 + z], in_sem.at[z]
        )
        for z in range(LZ)
    ]
    for load in loads:
        load.start()

    barrier = pltpu.get_barrier_semaphore()
    pl.semaphore_signal(barrier, inc=1, device_id={"vblk": 1 - core}, device_id_type=MESH)

    def greet(d, carry):
        pl.semaphore_signal(
            barrier, inc=1, device_id={"slab": lax.rem(me + d, n)}, device_id_type=MESH
        )
        return carry

    lax.fori_loop(1, n, greet, 0)

    @pl.when(jnp.logical_not(has_down))
    def _():
        link_z[...] = jnp.zeros_like(link_z)
        for field in fields[:2]:
            field[:, :, 0] = jnp.zeros(field.shape[:2] + field.shape[3:], jnp.float32)

    for edge in (0, LZ + 1):
        e_filt[:, :, edge] = jnp.zeros(e_filt.shape[:2] + e_filt.shape[3:], jnp.float32)

    @pl.when(jnp.logical_not(has_up))
    def _():
        for field in fields[:2]:
            field[:, :, LZ + 1] = jnp.zeros(field.shape[:2] + field.shape[3:], jnp.float32)

    @pl.when(jnp.logical_not(has_prev))
    def _():
        link_y[...] = jnp.zeros_like(link_y)
        y_before[...] = jnp.zeros_like(y_before)

    @pl.when(jnp.logical_not(has_next))
    def _():
        y_after[...] = jnp.zeros_like(y_after)

    for load in loads:
        load.wait()
    pl.semaphore_wait(barrier, n)

    def halo(stage, kind, chunk):
        field = fields[stage]
        own = pl.ds(pl.multiple_of(chunk * CHUNK, CHUNK), CHUNK)
        up = pl.ds(LAYER - 128, 128) if stage == 2 else slice(None)
        down = pl.ds(0, 128) if stage == 2 else slice(None)
        middle = pl.ds(128, 128)
        src, dst, to = (
            (field.at[:, :, LZ, own, up], field.at[:, :, 0, own, up], me + GY),
            (field.at[:, :, 1, own, down], field.at[:, :, LZ + 1, own, down], me - GY),
            (
                field.at[:, :, pl.ds(1, LZ), own, pl.ds(0, 128)],
                y_after.at[stage, :, :, :, own],
                me - 1,
            ),
            (
                field.at[:, :, pl.ds(1, LZ), own, pl.ds(LAYER - 128, 128)],
                y_before.at[min(stage, 1), :, :, :, own],
                me + 1,
            ),
            (field.at[:, :, LZ, own, middle], field.at[:, :, 0, own, middle], me + GY),
            (field.at[:, :, 1, own, middle], field.at[:, :, LZ + 1, own, middle], me - GY),
        )[kind]
        return pltpu.make_async_remote_copy(
            src_ref=src, dst_ref=dst,
            send_sem=halo_send.at[stage, kind, chunk],
            recv_sem=halo_recv.at[stage, kind, chunk],
            device_id={"slab": to}, device_id_type=MESH,
        )

    sends = (has_up, has_down, has_prev, has_next, has_up & high_rows, has_down & low_rows)
    receives = (has_down, has_up, has_next, has_prev, has_down & high_rows, has_up & low_rows)
    kinds = ((0, 1, 2, 3), (0, 1, 2, 3), (0, 1, 4, 5, 2))

    def start_halo(stage, chunk):
        for kind in kinds[stage]:
            pl.when(sends[kind])(lambda kind=kind: halo(stage, kind, chunk).start())

    def await_halo(stage, chunk):
        for kind in kinds[stage]:
            pl.when(receives[kind])(lambda kind=kind: halo(stage, kind, chunk).wait_recv())

    def link_copy(index):
        if index < LZ:
            src = link_ref.at[1, :, pl.ds((index + 1) * LAYER - 128, 128)]
            dst, to = link_y.at[index], me + 1
        else:
            src = link_ref.at[2, :, pl.ds((LZ - 1) * LAYER, LAYER)]
            dst, to = link_z, me + GY
        return pltpu.make_async_remote_copy(
            src_ref=src, dst_ref=dst, send_sem=link_send.at[index],
            recv_sem=link_recv.at[index], device_id={"slab": to}, device_id_type=MESH,
        )

    def pair_copy(which, chunk):
        own = pl.ds(pl.multiple_of(chunk * CHUNK, CHUNK), CHUNK)
        src = e_filt.at[:, :, pl.ds(1, LZ), own] if which == 0 else b_own.at[:, :, :, own]
        dst = (f_other, b_other)[which].at[:, :, :, own]
        return pltpu.make_async_remote_copy(
            src_ref=src, dst_ref=dst, send_sem=pair_send.at[which, chunk],
            recv_sem=pair_recv.at[which, chunk],
            device_id={"vblk": 1 - core}, device_id_type=MESH,
        )

    def loop(body):
        def step(chunk, carry):
            body(chunk)
            return carry

        lax.fori_loop(0, chunks, step, 0)

    @pl.when(has_next)
    def _():
        for index in range(LZ):
            link_copy(index).start()

    @pl.when(has_up)
    def _():
        link_copy(LZ).start()

    loop(lambda chunk: start_halo(0, chunk))

    @pl.when(has_prev)
    def _():
        for index in range(LZ):
            link_copy(index).wait_recv()

    @pl.when(has_down)
    def _():
        link_copy(LZ).wait_recv()

    for z in range(LZ):
        lanes = pl.ds(z * LAYER, LAYER)
        forward = [link_ref[mu, :, lanes] for mu in range(3)]
        below = link_z[...] if z == 0 else link_ref[2, :, pl.ds((z - 1) * LAYER, LAYER)]
        backward = [x_backward(forward[0]), y_backward(forward[1], link_y[z]), below]
        for side, table in enumerate((forward, backward)):
            for mu in range(3):
                for k in range(18):
                    spread[side, mu, k, z] = jnp.broadcast_to(
                        table[mu][k : k + 1], (8, LAYER)
                    )

    def hop(stage, chunk, finish):
        field = fields[stage]
        both = stage < 2
        own = pl.ds(pl.multiple_of(chunk * CHUNK, CHUNK), CHUNK)

        def shift(z, carry):
            for part_id in range(2):
                for colour in range(3):
                    layer = field[part_id, colour, z + 1, own, :]
                    moved[0, part_id, colour, z] = x_forward(layer)
                    moved[1, part_id, colour, z] = y_forward(
                        layer, y_after[stage, part_id, colour, z, own, :]
                    )
                    if both:
                        moved[2, part_id, colour, z] = x_backward(layer)
                        moved[3, part_id, colour, z] = y_backward(
                            layer, y_before[stage, part_id, colour, z, own, :]
                        )
            return carry

        lax.fori_loop(0, LZ, shift, 0)

        def take(ref, *at):
            return ref[at].reshape(CHUNK // 8, 8, 128)

        def add_hops(pairs, z, lanes):
            acc_re = [None] * 3
            acc_im = [None] * 3
            for mu, side in pairs:
                if mu == 2:
                    here = [
                        take(field, c // 3, c % 3, z + (0 if side else 2), own, lanes)
                        for c in range(6)
                    ]
                else:
                    here = [
                        take(moved, 2 * side + mu, c // 3, c % 3, z, slice(None), lanes)
                        for c in range(6)
                    ]
                for row in range(3):
                    for col in range(3):
                        k = row * 3 + col if side == 0 else col * 3 + row
                        link_re = spread[side, mu, k, z, :, lanes]
                        link_im = spread[side, mu, 9 + k, z, :, lanes]
                        re, im = here[col], here[3 + col]
                        if side == 0:
                            real = link_re * re - link_im * im
                            imag = link_re * im + link_im * re
                        else:
                            real = link_re * re + link_im * im
                            imag = link_re * im - link_im * re
                        if acc_re[row] is None:
                            acc_re[row], acc_im[row] = real, imag
                        else:
                            acc_re[row] = acc_re[row] + real
                            acc_im[row] = acc_im[row] + imag
            return acc_re, acc_im

        def tile(index, carry):
            z = index // (LAYER // 128)
            lanes = pl.ds(pl.multiple_of(lax.rem(index, LAYER // 128) * 128, 128), 128)
            sides = (0, 1) if both else (0,)
            pairs = [(mu, side) for mu in range(3) for side in sides]
            sums_of = add_hops(pairs, z, lanes)
            for row in range(3):
                for part_id in range(2):
                    finish(part_id, row, z, own, lanes, sums_of[part_id][row])
            return carry

        def edge_tile(index, carry):
            lanes = pl.ds(pl.multiple_of(index * 128, 128), 128)
            sums_of = add_hops([(2, 1)], 0, lanes)
            for row in range(3):
                for part_id in range(2):
                    there = merged(b_own, part_id, row, 0, own, lanes)
                    finish(part_id, row, 0, own, lanes, there + sums_of[part_id][row])
            return carry

        lax.fori_loop(0, LZ * LAYER // 128, tile, 0)
        if not both:
            lax.fori_loop(0, LAYER // 128, edge_tile, 0)

    def merged(ref, part_id, row, z, own, lanes):
        return ref[part_id, row, z, own, lanes].reshape(CHUNK // 8, 8, 128)

    def finish_first(part_id, row, z, own, lanes, value):
        center = merged(e_v, part_id, row, z + 1, own, lanes)
        done = (OWN * center - value) * (1.0 / half_width)
        e_first[part_id, row, z + 1, own, lanes] = done.reshape(CHUNK, 128)

    def finish_filtered(part_id, row, z, own, lanes, value):
        center = merged(e_first, part_id, row, z + 1, own, lanes)
        start = merged(e_v, part_id, row, z + 1, own, lanes)
        done = (OWN * center - value) * (2.0 / half_width) - start
        e_filt[part_id, row, z + 1, own, lanes] = done.reshape(CHUNK, 128)

    def finish_bonds(part_id, row, z, own, lanes, value):
        b_own[part_id, row, z, own, lanes] = value.reshape(CHUNK, 128)

    def do_first(chunk):
        await_halo(0, chunk)
        hop(0, chunk, finish_first)
        start_halo(1, chunk)

    def do_filtered(chunk):
        await_halo(1, chunk)
        hop(1, chunk, finish_filtered)
        pair_copy(0, chunk).start()
        start_halo(2, chunk)

    def do_bonds(chunk):
        await_halo(2, chunk)
        hop(2, chunk, finish_bonds)
        pair_copy(1, chunk).start()

    loop(do_first)
    loop(do_filtered)
    loop(lambda chunk: pair_copy(0, chunk).wait_recv())

    def stacked(ref, colour, z):
        return halves(jnp.concatenate([ref[0, colour, z], ref[1, colour, z]], axis=0))

    lane_dims = ((1,), (1,))
    sums[...] = jnp.zeros_like(sums)
    turn = [halves(turn_ref[side]) for side in range(2)]

    for colour in range(3):
        for z in range(LZ):
            mine = stacked(e_filt, colour, z + 1)
            other = stacked(f_other, colour, z)
            sums[0] += split_dot(mine, mine, lane_dims)
            sums[1] += split_dot(other, mine, lane_dims)
            turned = split_dot(turn[0], mine, ((1,), (0,)))
            turned = turned + split_dot(turn[1], other, ((1,), (0,)))
            for part_id in range(2):
                out_ref[part_id, colour, :, pl.ds(z * LAYER, LAYER)] = turned[
                    part_id * count : (part_id + 1) * count
                ]

    loop(do_bonds)
    loop(lambda chunk: pair_copy(1, chunk).wait_recv())

    for colour in range(3):
        for z in range(LZ):
            mine = stacked(e_filt, colour, z + 1)
            other = stacked(f_other, colour, z)
            bond = stacked(b_own, colour, z)
            bond_other = stacked(b_other, colour, z)
            sums[2] += split_dot(mine, bond, lane_dims) + split_dot(bond, mine, lane_dims)
            sums[3] += split_dot(other, bond, lane_dims) + split_dot(bond_other, mine, lane_dims)

    def inner(index):
        top = sums[index, pl.ds(0, count), :]
        low = sums[index, pl.ds(count, count), :]
        return (
            top[:, :count] + low[:, count:],
            top[:, count:] - low[:, :count],
        )

    sites = 3.0 * n * vec_ref.shape[3]
    spare = 128 - count
    full = 8 * count // 128
    blocks = []
    for side in range(2):
        gram = inner(side)
        hopped = inner(2 + side)
        for part_id in range(2):
            projected = (OWN * gram[part_id] - hopped[part_id]) * (1.0 / half_width)
            blocks += [gram[part_id] * (1.0 / sites), projected * (1.0 / sites)]
    tail = jnp.concatenate(blocks[full:], axis=1)
    for index in range(full):
        part[pl.ds(index * count, count), :] = jnp.concatenate(
            [blocks[index], tail[:, index * spare : (index + 1) * spare]], axis=1
        )
    if part.shape[0] > full * count:
        left = part.shape[0] - full * count
        part[pl.ds(full * count, left), :] = jnp.zeros((left, 128), jnp.float32)

    def rows_of(owner):
        return pl.ds(pl.multiple_of(owner * rows, 8), rows)

    def part_copy(d):
        owner = lax.rem(me + d, n)
        return pltpu.make_async_remote_copy(
            src_ref=part.at[rows_of(owner)],
            dst_ref=slots.at[d], send_sem=part_send.at[d], recv_sem=part_recv.at[d],
            device_id={"slab": owner}, device_id_type=MESH,
        )

    def total_copy(d, source):
        return pltpu.make_async_remote_copy(
            src_ref=total.at[rows_of(source)], dst_ref=total.at[rows_of(source)],
            send_sem=total_send.at[d], recv_sem=total_recv.at[d],
            device_id={"slab": lax.rem(me + d, n)}, device_id_type=MESH,
        )

    def around(body):
        def step(d, carry):
            body(d)
            return carry

        lax.fori_loop(1, n, step, 0)

    around(lambda d: part_copy(d).start())
    around(lambda d: part_copy(d).wait_recv())
    total[rows_of(me), :] = lax.fori_loop(
        1, n, lambda d, running: running + slots[d], part[rows_of(me), :]
    )
    around(lambda d: total_copy(d, me).start())
    around(lambda d: total_copy(d, lax.rem(me + n - d, n)).wait_recv())

    packed = [total[pl.ds(index * count, count), :] for index in range(full)]
    tail = jnp.concatenate([block[:, count:] for block in packed], axis=1)
    found = [block[:, :count] for block in packed]
    found += [tail[:, i * count : (i + 1) * count] for i in range(8 - full)]
    for side, at in ((0, core), (1, 1 - core)):
        own_rows = pl.ds(pl.multiple_of(at * count, 8), count)
        for part_id in range(2):
            gram_ref[part_id, own_rows, :] = found[4 * side + 2 * part_id]
            proj_ref[part_id, own_rows, :] = found[4 * side + 2 * part_id + 1]

    def end_sends(chunk):
        for stage in range(3):
            for kind in kinds[stage]:
                pl.when(sends[kind])(
                    lambda stage=stage, kind=kind: halo(stage, kind, chunk).wait_send()
                )
        for which in range(2):
            pair_copy(which, chunk).wait_send()

    loop(end_sends)

    @pl.when(has_next)
    def _():
        for index in range(LZ):
            link_copy(index).wait_send()

    @pl.when(has_up)
    def _():
        link_copy(LZ).wait_send()

    around(lambda d: part_copy(d).wait_send())
    around(lambda d: total_copy(d, me).wait_send())


def per_device(n, vectors, links, rotation):
    count, local_sites = vectors.shape[2], vectors.shape[3]
    core = lax.axis_index("vblk")
    link_rows = links.reshape(2, 3, 3, 3, local_sites)
    link_rows = jnp.transpose(link_rows, (2, 0, 1, 3, 4)).reshape(3, 18, local_sites)
    columns = lax.dynamic_slice_in_dim(rotation, core * count, count, 2)
    columns = jnp.swapaxes(columns, 1, 2)
    blocks = []
    for side in (core, 1 - core):
        own = lax.dynamic_slice_in_dim(columns, side * count, count, 2)
        top = jnp.concatenate([own[0], -own[1]], axis=1)
        low = jnp.concatenate([own[1], own[0]], axis=1)
        blocks.append(jnp.concatenate([top, low], axis=0))
    turn = jnp.stack(blocks)

    chunks = count // CHUNK
    rows = 8 * -(-8 * count * count // (128 * 8 * n))
    all_rows = n * rows
    f32 = jnp.float32
    halo_shape = (2, 3, LZ + 2, count, LAYER)
    block = (2, 3, LZ, count, LAYER)
    vmem = pl.BlockSpec(memory_space=pltpu.VMEM)
    return pl.pallas_call(
        functools.partial(kernel, n, rows),
        out_shape=(
            jax.ShapeDtypeStruct(vectors.shape, f32),
            jax.ShapeDtypeStruct((2, 2 * count, count), f32),
            jax.ShapeDtypeStruct((2, 2 * count, count), f32),
        ),
        in_specs=[pl.BlockSpec(memory_space=pl.ANY), vmem, vmem],
        out_specs=(vmem, vmem, vmem),
        scratch_shapes=[
            pltpu.VMEM(halo_shape, f32),
            pltpu.VMEM(halo_shape, f32),
            pltpu.VMEM(halo_shape, f32),
            pltpu.VMEM((2, 2, 3, LZ, count, 128), f32),
            pltpu.VMEM((3, 2, 3, LZ, count, 128), f32),
            pltpu.VMEM((LZ, 18, 128), f32),
            pltpu.VMEM((18, LAYER), f32),
            pltpu.VMEM((2, 3, 18, LZ, 8, LAYER), f32),
            pltpu.VMEM((4, 2, 3, LZ, CHUNK, LAYER), f32),
            pltpu.VMEM(block, f32),
            pltpu.VMEM(block, f32),
            pltpu.VMEM(block, f32),
            pltpu.VMEM((4, 2 * count, 2 * count), f32),
            pltpu.VMEM((all_rows, 128), f32),
            pltpu.VMEM((n, rows, 128), f32),
            pltpu.VMEM((all_rows, 128), f32),
            pltpu.SemaphoreType.DMA((LZ,)),
            pltpu.SemaphoreType.DMA((3, 6, chunks)),
            pltpu.SemaphoreType.DMA((3, 6, chunks)),
            pltpu.SemaphoreType.DMA((LZ + 1,)),
            pltpu.SemaphoreType.DMA((LZ + 1,)),
            pltpu.SemaphoreType.DMA((2, chunks)),
            pltpu.SemaphoreType.DMA((2, chunks)),
            pltpu.SemaphoreType.DMA((n,)),
            pltpu.SemaphoreType.DMA((n,)),
            pltpu.SemaphoreType.DMA((n,)),
            pltpu.SemaphoreType.DMA((n,)),
        ],
        compiler_params=pltpu.CompilerParams(
            collective_id=0, has_side_effects=True, vmem_limit_bytes=56 * 1024 * 1024
        ),
    )(vectors, link_rows, turn)


def solution(mesh):
    in_specs = (
        P(None, None, "vblk", ("parts", "slab")),
        P(None, None, None, ("parts", "slab")),
        P(),
    )
    out_specs = (
        P(None, None, "vblk", ("parts", "slab")),
        P("parts", None, "vblk"),
        P("parts", None, "vblk"),
    )
    return jax.shard_map(
        functools.partial(per_device, mesh.shape["slab"]),
        mesh=mesh, in_specs=in_specs, out_specs=out_specs, check_vma=False,
    )
```

```python
import functools

import jax
import jax.numpy as jnp
from jax import lax
from jax.experimental import pallas as pl
from jax.experimental.pallas import tpu as pltpu
from jax.sharding import PartitionSpec as P

LX = 96
LY = 4
LZ = 2
GY = 4
LAYER = LY * LX
CHUNK = 16
MESH = pl.DeviceIdType.MESH

center_shift = 8.0
half_width = 6.0
OWN = 6.0 - center_shift


def edge_mask(shape, x):
    lane = lax.broadcasted_iota(jnp.int32, shape, 1)
    mask = lane == x
    for row in range(1, LY):
        mask = mask | (lane == row * LX + x)
    return mask


def x_forward(layer):
    return jnp.where(
        edge_mask(layer.shape, LX - 1),
        pltpu.roll(layer, LX - 1, 1),
        pltpu.roll(layer, LAYER - 1, 1),
    )


def x_backward(layer):
    return jnp.where(
        edge_mask(layer.shape, 0),
        pltpu.roll(layer, LAYER - LX + 1, 1),
        pltpu.roll(layer, 1, 1),
    )


def y_forward(layer, after):
    joined = jnp.concatenate([layer, after], axis=1)
    return pltpu.roll(joined, LAYER + 128 - LX, 1)[:, :LAYER]


def y_backward(layer, before):
    joined = jnp.concatenate([before, layer], axis=1)
    return pltpu.roll(joined, LAYER + LX, 1)[:, :LAYER]


def halves(x):
    high = x.astype(jnp.bfloat16)
    low = (x - high.astype(jnp.float32)).astype(jnp.bfloat16)
    return high, low


def split_dot(left, right, dims):
    dot = functools.partial(
        lax.dot_general, dimension_numbers=(dims, ((), ())), preferred_element_type=jnp.float32
    )
    return dot(left[0], right[0]) + (dot(left[0], right[1]) + dot(left[1], right[0]))


def kernel(
    n, rows, vec_ref, raw_ref, turn_ref, result_ref, gram_ref, proj_ref,
    e_v, e_first, e_filt, y_before, y_after, link_y, link_z, spread, moved,
    f_other, b_own, b_other, sums, part, slots, total,
    in_sem, halo_send, halo_recv, link_send, link_recv, pair_send, pair_recv,
    part_send, part_recv, total_send, total_recv, link_ref, columns, out_ref, out_sem,
):
    me = lax.axis_index("slab")
    core = lax.axis_index("vblk")
    count = vec_ref.shape[2]
    chunks = count // CHUNK
    row_pos = lax.rem(me, GY)
    has_up = me + GY < n
    has_down = me >= GY
    has_next = row_pos < GY - 1
    has_prev = row_pos > 0
    fields = (e_v, e_first, e_filt)
    low_rows = row_pos < GY // 2
    high_rows = jnp.logical_not(low_rows)

    loads = [
        pltpu.make_async_copy(
            vec_ref.at[:, :, :, pl.ds(z * LAYER, LAYER)], e_v.at[:, :, 1 + z], in_sem.at[z]
        )
        for z in range(LZ)
    ]
    for load in loads:
        load.start()

    barrier = pltpu.get_barrier_semaphore()
    pl.semaphore_signal(barrier, inc=1, device_id={"vblk": 1 - core}, device_id_type=MESH)

    def greet(d, carry):
        pl.semaphore_signal(
            barrier, inc=1, device_id={"slab": lax.rem(me + d, n)}, device_id_type=MESH
        )
        return carry

    lax.fori_loop(1, n, greet, 0)

    for mu in range(3):
        for row in range(3):
            for col in range(3):
                for c in range(2):
                    link_ref[mu, pl.ds(9 * c + 3 * row + col, 1), :] = raw_ref[
                        row, 3 * mu + col, pl.ds(c, 1), :
                    ]

    @pl.when(jnp.logical_not(has_down))
    def _():
        link_z[...] = jnp.zeros_like(link_z)
        for field in fields[:2]:
            field[:, :, 0] = jnp.zeros(field.shape[:2] + field.shape[3:], jnp.float32)

    for edge in (0, LZ + 1):
        e_filt[:, :, edge] = jnp.zeros(e_filt.shape[:2] + e_filt.shape[3:], jnp.float32)

    @pl.when(jnp.logical_not(has_up))
    def _():
        for field in fields[:2]:
            field[:, :, LZ + 1] = jnp.zeros(field.shape[:2] + field.shape[3:], jnp.float32)

    @pl.when(jnp.logical_not(has_prev))
    def _():
        link_y[...] = jnp.zeros_like(link_y)
        y_before[...] = jnp.zeros_like(y_before)

    @pl.when(jnp.logical_not(has_next))
    def _():
        y_after[...] = jnp.zeros_like(y_after)

    for load in loads:
        load.wait()
    pl.semaphore_wait(barrier, n)

    def halo(stage, kind, chunk):
        field = fields[stage]
        own = pl.ds(pl.multiple_of(chunk * CHUNK, CHUNK), CHUNK)
        up = pl.ds(LAYER - 128, 128) if stage == 2 else slice(None)
        down = pl.ds(0, 128) if stage == 2 else slice(None)
        middle = pl.ds(128, 128)
        src, dst, to = (
            (field.at[:, :, LZ, own, up], field.at[:, :, 0, own, up], me + GY),
            (field.at[:, :, 1, own, down], field.at[:, :, LZ + 1, own, down], me - GY),
            (
                field.at[:, :, pl.ds(1, LZ), own, pl.ds(0, 128)],
                y_after.at[stage, :, :, :, own],
                me - 1,
            ),
            (
                field.at[:, :, pl.ds(1, LZ), own, pl.ds(LAYER - 128, 128)],
                y_before.at[min(stage, 1), :, :, :, own],
                me + 1,
            ),
            (field.at[:, :, LZ, own, middle], field.at[:, :, 0, own, middle], me + GY),
            (field.at[:, :, 1, own, middle], field.at[:, :, LZ + 1, own, middle], me - GY),
        )[kind]
        return pltpu.make_async_remote_copy(
            src_ref=src, dst_ref=dst,
            send_sem=halo_send.at[stage, kind, chunk],
            recv_sem=halo_recv.at[stage, kind, chunk],
            device_id={"slab": to}, device_id_type=MESH,
        )

    sends = (has_up, has_down, has_prev, has_next, has_up & high_rows, has_down & low_rows)
    receives = (has_down, has_up, has_next, has_prev, has_down & high_rows, has_up & low_rows)
    kinds = ((0, 1, 2, 3), (0, 1, 2, 3), (0, 1, 4, 5, 2))

    def start_halo(stage, chunk):
        for kind in kinds[stage]:
            pl.when(sends[kind])(lambda kind=kind: halo(stage, kind, chunk).start())

    def await_halo(stage, chunk):
        for kind in kinds[stage]:
            pl.when(receives[kind])(lambda kind=kind: halo(stage, kind, chunk).wait_recv())

    def link_copy(index):
        if index < LZ:
            src = link_ref.at[1, :, pl.ds((index + 1) * LAYER - 128, 128)]
            dst, to = link_y.at[index], me + 1
        else:
            src = link_ref.at[2, :, pl.ds((LZ - 1) * LAYER, LAYER)]
            dst, to = link_z, me + GY
        return pltpu.make_async_remote_copy(
            src_ref=src, dst_ref=dst, send_sem=link_send.at[index],
            recv_sem=link_recv.at[index], device_id={"slab": to}, device_id_type=MESH,
        )

    def pair_copy(which, chunk):
        own = pl.ds(pl.multiple_of(chunk * CHUNK, CHUNK), CHUNK)
        src = e_filt.at[:, :, pl.ds(1, LZ), own] if which == 0 else b_own.at[:, :, :, own]
        dst = (f_other, b_other)[which].at[:, :, :, own]
        return pltpu.make_async_remote_copy(
            src_ref=src, dst_ref=dst, send_sem=pair_send.at[which, chunk],
            recv_sem=pair_recv.at[which, chunk],
            device_id={"vblk": 1 - core}, device_id_type=MESH,
        )

    def loop(body):
        def step(chunk, carry):
            body(chunk)
            return carry

        lax.fori_loop(0, chunks, step, 0)

    @pl.when(has_next)
    def _():
        for index in range(LZ):
            link_copy(index).start()

    @pl.when(has_up)
    def _():
        link_copy(LZ).start()

    loop(lambda chunk: start_halo(0, chunk))

    @pl.when(has_prev)
    def _():
        for index in range(LZ):
            link_copy(index).wait_recv()

    @pl.when(has_down)
    def _():
        link_copy(LZ).wait_recv()

    for z in range(LZ):
        lanes = pl.ds(z * LAYER, LAYER)
        forward = [link_ref[mu, :, lanes] for mu in range(3)]
        below = link_z[...] if z == 0 else link_ref[2, :, pl.ds((z - 1) * LAYER, LAYER)]
        backward = [x_backward(forward[0]), y_backward(forward[1], link_y[z]), below]
        for side, table in enumerate((forward, backward)):
            for mu in range(3):
                for k in range(18):
                    spread[side, mu, k, z] = jnp.broadcast_to(
                        table[mu][k : k + 1], (8, LAYER)
                    )

    def hop(stage, chunk, finish):
        field = fields[stage]
        both = stage < 2
        own = pl.ds(pl.multiple_of(chunk * CHUNK, CHUNK), CHUNK)

        def shift(z, carry):
            for part_id in range(2):
                for colour in range(3):
                    layer = field[part_id, colour, z + 1, own, :]
                    moved[0, part_id, colour, z] = x_forward(layer)
                    moved[1, part_id, colour, z] = y_forward(
                        layer, y_after[stage, part_id, colour, z, own, :]
                    )
                    if both:
                        moved[2, part_id, colour, z] = x_backward(layer)
                        moved[3, part_id, colour, z] = y_backward(
                            layer, y_before[stage, part_id, colour, z, own, :]
                        )
            return carry

        lax.fori_loop(0, LZ, shift, 0)

        def take(ref, *at):
            return ref[at].reshape(CHUNK // 8, 8, 128)

        def add_hops(pairs, z, lanes):
            acc_re = [None] * 3
            acc_im = [None] * 3
            for mu, side in pairs:
                if mu == 2:
                    here = [
                        take(field, c // 3, c % 3, z + (0 if side else 2), own, lanes)
                        for c in range(6)
                    ]
                else:
                    here = [
                        take(moved, 2 * side + mu, c // 3, c % 3, z, slice(None), lanes)
                        for c in range(6)
                    ]
                for row in range(3):
                    for col in range(3):
                        k = row * 3 + col if side == 0 else col * 3 + row
                        link_re = spread[side, mu, k, z, :, lanes]
                        link_im = spread[side, mu, 9 + k, z, :, lanes]
                        re, im = here[col], here[3 + col]
                        if side == 0:
                            real = link_re * re - link_im * im
                            imag = link_re * im + link_im * re
                        else:
                            real = link_re * re + link_im * im
                            imag = link_re * im - link_im * re
                        if acc_re[row] is None:
                            acc_re[row], acc_im[row] = real, imag
                        else:
                            acc_re[row] = acc_re[row] + real
                            acc_im[row] = acc_im[row] + imag
            return acc_re, acc_im

        def tile(index, carry):
            z = index // (LAYER // 128)
            lanes = pl.ds(pl.multiple_of(lax.rem(index, LAYER // 128) * 128, 128), 128)
            sides = (0, 1) if both else (0,)
            pairs = [(mu, side) for mu in range(3) for side in sides]
            sums_of = add_hops(pairs, z, lanes)
            for row in range(3):
                for part_id in range(2):
                    finish(part_id, row, z, own, lanes, sums_of[part_id][row])
            return carry

        def edge_tile(index, carry):
            lanes = pl.ds(pl.multiple_of(index * 128, 128), 128)
            sums_of = add_hops([(2, 1)], 0, lanes)
            for row in range(3):
                for part_id in range(2):
                    there = merged(b_own, part_id, row, 0, own, lanes)
                    finish(part_id, row, 0, own, lanes, there + sums_of[part_id][row])
            return carry

        lax.fori_loop(0, LZ * LAYER // 128, tile, 0)
        if not both:
            lax.fori_loop(0, LAYER // 128, edge_tile, 0)

    def merged(ref, part_id, row, z, own, lanes):
        return ref[part_id, row, z, own, lanes].reshape(CHUNK // 8, 8, 128)

    def finish_first(part_id, row, z, own, lanes, value):
        center = merged(e_v, part_id, row, z + 1, own, lanes)
        done = (OWN * center - value) * (1.0 / half_width)
        e_first[part_id, row, z + 1, own, lanes] = done.reshape(CHUNK, 128)

    def finish_filtered(part_id, row, z, own, lanes, value):
        center = merged(e_first, part_id, row, z + 1, own, lanes)
        start = merged(e_v, part_id, row, z + 1, own, lanes)
        done = (OWN * center - value) * (2.0 / half_width) - start
        e_filt[part_id, row, z + 1, own, lanes] = done.reshape(CHUNK, 128)

    def finish_bonds(part_id, row, z, own, lanes, value):
        b_own[part_id, row, z, own, lanes] = value.reshape(CHUNK, 128)

    def do_first(chunk):
        await_halo(0, chunk)
        hop(0, chunk, finish_first)
        start_halo(1, chunk)

    def do_filtered(chunk):
        await_halo(1, chunk)
        hop(1, chunk, finish_filtered)
        pair_copy(0, chunk).start()
        start_halo(2, chunk)

    def do_bonds(chunk):
        await_halo(2, chunk)
        hop(2, chunk, finish_bonds)
        pair_copy(1, chunk).start()

    for c in range(2):

        @pl.when(core == c)
        def _(c=c):
            columns[...] = turn_ref[:, :, pl.ds(c * count, count)]

    loop(do_first)
    loop(do_filtered)
    loop(lambda chunk: pair_copy(0, chunk).wait_recv())

    def stacked(ref, colour, z):
        return halves(jnp.concatenate([ref[0, colour, z], ref[1, colour, z]], axis=0))

    lane_dims = ((1,), (1,))
    sums[...] = jnp.zeros_like(sums)
    turn = []
    for at in (core, 1 - core):
        real, imag = [
            columns[c, pl.ds(pl.multiple_of(at * count, 8), count), :] for c in range(2)
        ]
        left = jnp.concatenate(
            [jnp.concatenate([real, imag], 1), jnp.concatenate([-imag, real], 1)], 0
        )
        turn.append(halves(left))

    for colour in range(3):
        for z in range(LZ):
            mine = stacked(e_filt, colour, z + 1)
            other = stacked(f_other, colour, z)
            sums[0] += split_dot(mine, mine, lane_dims)
            sums[1] += split_dot(other, mine, lane_dims)
            turned = split_dot(turn[0], mine, ((0,), (0,)))
            turned = turned + split_dot(turn[1], other, ((0,), (0,)))
            for part_id in range(2):
                out_ref[part_id, colour, :, pl.ds(z * LAYER, LAYER)] = turned[
                    part_id * count : (part_id + 1) * count
                ]

    result = pltpu.make_async_copy(out_ref, result_ref, out_sem)
    result.start()
    loop(do_bonds)

    for colour in range(3):
        for z in range(LZ):
            mine = stacked(e_filt, colour, z + 1)
            other = stacked(f_other, colour, z)
            bond = stacked(b_own, colour, z)
            sums[2] += split_dot(mine, bond, lane_dims) + split_dot(bond, mine, lane_dims)
            sums[3] += split_dot(other, bond, lane_dims)

    loop(lambda chunk: pair_copy(1, chunk).wait_recv())

    for colour in range(3):
        for z in range(LZ):
            mine = stacked(e_filt, colour, z + 1)
            bond_other = stacked(b_other, colour, z)
            sums[3] += split_dot(bond_other, mine, lane_dims)

    def inner(index):
        top = sums[index, pl.ds(0, count), :]
        low = sums[index, pl.ds(count, count), :]
        return (
            top[:, :count] + low[:, count:],
            top[:, count:] - low[:, :count],
        )

    sites = 3.0 * n * vec_ref.shape[3]
    spare = 128 - count
    full = 8 * count // 128
    blocks = []
    for side in range(2):
        gram = inner(side)
        hopped = inner(2 + side)
        for part_id in range(2):
            projected = (OWN * gram[part_id] - hopped[part_id]) * (1.0 / half_width)
            blocks += [gram[part_id] * (1.0 / sites), projected * (1.0 / sites)]
    tail = jnp.concatenate(blocks[full:], axis=1)
    for index in range(full):
        part[pl.ds(index * count, count), :] = jnp.concatenate(
            [blocks[index], tail[:, index * spare : (index + 1) * spare]], axis=1
        )
    if part.shape[0] > full * count:
        left = part.shape[0] - full * count
        part[pl.ds(full * count, left), :] = jnp.zeros((left, 128), jnp.float32)

    def rows_of(owner):
        return pl.ds(pl.multiple_of(owner * rows, 8), rows)

    def part_copy(d):
        owner = lax.rem(me + d, n)
        return pltpu.make_async_remote_copy(
            src_ref=part.at[rows_of(owner)],
            dst_ref=slots.at[d], send_sem=part_send.at[d], recv_sem=part_recv.at[d],
            device_id={"slab": owner}, device_id_type=MESH,
        )

    def total_copy(d, source):
        return pltpu.make_async_remote_copy(
            src_ref=total.at[rows_of(source)], dst_ref=total.at[rows_of(source)],
            send_sem=total_send.at[d], recv_sem=total_recv.at[d],
            device_id={"slab": lax.rem(me + d, n)}, device_id_type=MESH,
        )

    def around(body):
        def step(d, carry):
            body(d)
            return carry

        lax.fori_loop(1, n, step, 0)

    around(lambda d: part_copy(d).start())
    around(lambda d: part_copy(d).wait_recv())
    total[rows_of(me), :] = lax.fori_loop(
        1, n, lambda d, running: running + slots[d], part[rows_of(me), :]
    )
    around(lambda d: total_copy(d, me).start())
    around(lambda d: total_copy(d, lax.rem(me + n - d, n)).wait_recv())

    packed = [total[pl.ds(index * count, count), :] for index in range(full)]
    tail = jnp.concatenate([block[:, count:] for block in packed], axis=1)
    found = [block[:, :count] for block in packed]
    found += [tail[:, i * count : (i + 1) * count] for i in range(8 - full)]
    for side, at in ((0, core), (1, 1 - core)):
        own_rows = pl.ds(pl.multiple_of(at * count, 8), count)
        for part_id in range(2):
            gram_ref[part_id, own_rows, :] = found[4 * side + 2 * part_id]
            proj_ref[part_id, own_rows, :] = found[4 * side + 2 * part_id + 1]

    def end_sends(chunk):
        for stage in range(3):
            for kind in kinds[stage]:
                pl.when(sends[kind])(
                    lambda stage=stage, kind=kind: halo(stage, kind, chunk).wait_send()
                )
        for which in range(2):
            pair_copy(which, chunk).wait_send()

    loop(end_sends)

    @pl.when(has_next)
    def _():
        for index in range(LZ):
            link_copy(index).wait_send()

    @pl.when(has_up)
    def _():
        link_copy(LZ).wait_send()

    around(lambda d: part_copy(d).wait_send())
    around(lambda d: total_copy(d, me).wait_send())
    result.wait()


def per_device(n, vectors, links, rotation):
    count, local_sites = vectors.shape[2], vectors.shape[3]
    chunks = count // CHUNK
    rows = 8 * -(-8 * count * count // (128 * 8 * n))
    all_rows = n * rows
    f32 = jnp.float32
    halo_shape = (2, 3, LZ + 2, count, LAYER)
    block = (2, 3, LZ, count, LAYER)
    vmem = pl.BlockSpec(memory_space=pltpu.VMEM)
    return pl.pallas_call(
        functools.partial(kernel, n, rows),
        out_shape=(
            jax.ShapeDtypeStruct(vectors.shape, f32),
            jax.ShapeDtypeStruct((2, 2 * count, count), f32),
            jax.ShapeDtypeStruct((2, 2 * count, count), f32),
        ),
        in_specs=[pl.BlockSpec(memory_space=pl.ANY), vmem, vmem],
        out_specs=(pl.BlockSpec(memory_space=pl.ANY), vmem, vmem),
        scratch_shapes=[
            pltpu.VMEM(halo_shape, f32),
            pltpu.VMEM(halo_shape, f32),
            pltpu.VMEM(halo_shape, f32),
            pltpu.VMEM((2, 2, 3, LZ, count, 128), f32),
            pltpu.VMEM((3, 2, 3, LZ, count, 128), f32),
            pltpu.VMEM((LZ, 18, 128), f32),
            pltpu.VMEM((18, LAYER), f32),
            pltpu.VMEM((2, 3, 18, LZ, 8, LAYER), f32),
            pltpu.VMEM((4, 2, 3, LZ, CHUNK, LAYER), f32),
            pltpu.VMEM(block, f32),
            pltpu.VMEM(block, f32),
            pltpu.VMEM(block, f32),
            pltpu.VMEM((4, 2 * count, 2 * count), f32),
            pltpu.VMEM((all_rows, 128), f32),
            pltpu.VMEM((n, rows, 128), f32),
            pltpu.VMEM((all_rows, 128), f32),
            pltpu.SemaphoreType.DMA((LZ,)),
            pltpu.SemaphoreType.DMA((3, 6, chunks)),
            pltpu.SemaphoreType.DMA((3, 6, chunks)),
            pltpu.SemaphoreType.DMA((LZ + 1,)),
            pltpu.SemaphoreType.DMA((LZ + 1,)),
            pltpu.SemaphoreType.DMA((2, chunks)),
            pltpu.SemaphoreType.DMA((2, chunks)),
            pltpu.SemaphoreType.DMA((n,)),
            pltpu.SemaphoreType.DMA((n,)),
            pltpu.SemaphoreType.DMA((n,)),
            pltpu.SemaphoreType.DMA((n,)),
            pltpu.VMEM((3, 18, local_sites), f32),
            pltpu.VMEM((2, 2 * count, count), f32),
            pltpu.VMEM(vectors.shape, f32),
            pltpu.SemaphoreType.DMA,
        ],
        compiler_params=pltpu.CompilerParams(
            collective_id=0, has_side_effects=True, vmem_limit_bytes=56 * 1024 * 1024
        ),
    )(vectors, jnp.transpose(links, (1, 2, 0, 3)), rotation)


def solution(mesh):
    in_specs = (
        P(None, None, "vblk", ("parts", "slab")),
        P(None, None, None, ("parts", "slab")),
        P(),
    )
    out_specs = (
        P(None, None, "vblk", ("parts", "slab")),
        P("parts", None, "vblk"),
        P("parts", None, "vblk"),
    )
    return jax.shard_map(
        functools.partial(per_device, mesh.shape["slab"]),
        mesh=mesh, in_specs=in_specs, out_specs=out_specs, check_vma=False,
    )
```

```python
import functools

import jax
import jax.numpy as jnp
from jax import lax
from jax.experimental import pallas as pl
from jax.experimental.pallas import tpu as pltpu
from jax.sharding import PartitionSpec as P

LX = 96
LY = 4
LZ = 2
GY = 4
LAYER = LY * LX
CHUNK = 16
MESH = pl.DeviceIdType.MESH

center_shift = 8.0
half_width = 6.0
OWN = 6.0 - center_shift


def edge_mask(shape, x):
    lane = lax.broadcasted_iota(jnp.int32, shape, 1)
    mask = lane == x
    for row in range(1, LY):
        mask = mask | (lane == row * LX + x)
    return mask


def x_forward(layer):
    return jnp.where(
        edge_mask(layer.shape, LX - 1),
        pltpu.roll(layer, LX - 1, 1),
        pltpu.roll(layer, LAYER - 1, 1),
    )


def x_backward(layer):
    return jnp.where(
        edge_mask(layer.shape, 0),
        pltpu.roll(layer, LAYER - LX + 1, 1),
        pltpu.roll(layer, 1, 1),
    )


def y_forward(layer, after):
    joined = jnp.concatenate([layer, after], axis=1)
    return pltpu.roll(joined, LAYER + 128 - LX, 1)[:, :LAYER]


def y_backward(layer, before):
    joined = jnp.concatenate([before, layer], axis=1)
    return pltpu.roll(joined, LAYER + LX, 1)[:, :LAYER]


def halves(x):
    high = x.astype(jnp.bfloat16)
    low = (x - high.astype(jnp.float32)).astype(jnp.bfloat16)
    return high, low


def split_dot(left, right, dims):
    dot = functools.partial(
        lax.dot_general, dimension_numbers=(dims, ((), ())), preferred_element_type=jnp.float32
    )
    return dot(left[0], right[0]) + (dot(left[0], right[1]) + dot(left[1], right[0]))


def kernel(
    n, rows, vec_ref, raw_ref, turn_ref, result_ref, gram_ref, proj_ref,
    e_v, e_first, e_filt, y_before, y_after, link_y, link_z, spread, moved,
    f_other, b_own, b_other, sums, part, slots, total,
    in_sem, halo_send, halo_recv, link_send, link_recv, pair_send, pair_recv,
    part_send, part_recv, total_send, total_recv, link_ref, columns, out_ref, out_sem,
):
    me = lax.axis_index("slab")
    core = lax.axis_index("vblk")
    count = vec_ref.shape[2]
    chunks = count // CHUNK
    row_pos = lax.rem(me, GY)
    has_up = me + GY < n
    has_down = me >= GY
    has_next = row_pos < GY - 1
    has_prev = row_pos > 0
    fields = (e_v, e_first, e_filt)
    low_rows = row_pos < GY // 2
    high_rows = jnp.logical_not(low_rows)

    loads = [
        pltpu.make_async_copy(
            vec_ref.at[:, :, :, pl.ds(z * LAYER, LAYER)], e_v.at[:, :, 1 + z], in_sem.at[z]
        )
        for z in range(LZ)
    ]
    for load in loads:
        load.start()

    barrier = pltpu.get_barrier_semaphore()
    pl.semaphore_signal(barrier, inc=1, device_id={"vblk": 1 - core}, device_id_type=MESH)

    def greet(d, carry):
        pl.semaphore_signal(
            barrier, inc=1, device_id={"slab": lax.rem(me + d, n)}, device_id_type=MESH
        )
        return carry

    lax.fori_loop(1, n, greet, 0)

    for mu in range(3):
        for row in range(3):
            for col in range(3):
                for c in range(2):
                    link_ref[mu, pl.ds(9 * c + 3 * row + col, 1), :] = raw_ref[
                        row, 3 * mu + col, pl.ds(c, 1), :
                    ]

    @pl.when(jnp.logical_not(has_down))
    def _():
        link_z[...] = jnp.zeros_like(link_z)
        for field in fields[:2]:
            field[:, :, 0] = jnp.zeros(field.shape[:2] + field.shape[3:], jnp.float32)

    for edge in (0, LZ + 1):
        e_filt[:, :, edge] = jnp.zeros(e_filt.shape[:2] + e_filt.shape[3:], jnp.float32)

    @pl.when(jnp.logical_not(has_up))
    def _():
        for field in fields[:2]:
            field[:, :, LZ + 1] = jnp.zeros(field.shape[:2] + field.shape[3:], jnp.float32)

    @pl.when(jnp.logical_not(has_prev))
    def _():
        link_y[...] = jnp.zeros_like(link_y)
        y_before[...] = jnp.zeros_like(y_before)

    @pl.when(jnp.logical_not(has_next))
    def _():
        y_after[...] = jnp.zeros_like(y_after)

    for load in loads:
        load.wait()
    pl.semaphore_wait(barrier, n)

    def halo(stage, kind, chunk):
        field = fields[stage]
        own = pl.ds(pl.multiple_of(chunk * CHUNK, CHUNK), CHUNK)
        up = pl.ds(LAYER - 128, 128) if stage == 2 else slice(None)
        down = pl.ds(0, 128) if stage == 2 else slice(None)
        middle = pl.ds(128, 128)
        src, dst, to = (
            (field.at[:, :, LZ, own, up], field.at[:, :, 0, own, up], me + GY),
            (field.at[:, :, 1, own, down], field.at[:, :, LZ + 1, own, down], me - GY),
            (
                field.at[:, :, pl.ds(1, LZ), own, pl.ds(0, 128)],
                y_after.at[stage, :, :, :, own],
                me - 1,
            ),
            (
                field.at[:, :, pl.ds(1, LZ), own, pl.ds(LAYER - 128, 128)],
                y_before.at[min(stage, 1), :, :, :, own],
                me + 1,
            ),
            (field.at[:, :, LZ, own, middle], field.at[:, :, 0, own, middle], me + GY),
            (field.at[:, :, 1, own, middle], field.at[:, :, LZ + 1, own, middle], me - GY),
        )[kind]
        return pltpu.make_async_remote_copy(
            src_ref=src, dst_ref=dst,
            send_sem=halo_send.at[stage, kind, chunk],
            recv_sem=halo_recv.at[stage, kind, chunk],
            device_id={"slab": to}, device_id_type=MESH,
        )

    sends = (has_up, has_down, has_prev, has_next, has_up & high_rows, has_down & low_rows)
    receives = (has_down, has_up, has_next, has_prev, has_down & high_rows, has_up & low_rows)
    kinds = ((0, 1, 2, 3), (0, 1, 2, 3), (0, 1, 4, 5, 2))

    def start_halo(stage, chunk):
        for kind in kinds[stage]:
            pl.when(sends[kind])(lambda kind=kind: halo(stage, kind, chunk).start())

    def await_halo(stage, chunk):
        for kind in kinds[stage]:
            pl.when(receives[kind])(lambda kind=kind: halo(stage, kind, chunk).wait_recv())

    def link_copy(index):
        if index < LZ:
            src = link_ref.at[1, :, pl.ds((index + 1) * LAYER - 128, 128)]
            dst, to = link_y.at[index], me + 1
        else:
            src = link_ref.at[2, :, pl.ds((LZ - 1) * LAYER, LAYER)]
            dst, to = link_z, me + GY
        return pltpu.make_async_remote_copy(
            src_ref=src, dst_ref=dst, send_sem=link_send.at[index],
            recv_sem=link_recv.at[index], device_id={"slab": to}, device_id_type=MESH,
        )

    def pair_copy(which, chunk):
        own = pl.ds(pl.multiple_of(chunk * CHUNK, CHUNK), CHUNK)
        src = e_filt.at[:, :, pl.ds(1, LZ), own] if which == 0 else b_own.at[:, :, :, own]
        dst = (f_other, b_other)[which].at[:, :, :, own]
        return pltpu.make_async_remote_copy(
            src_ref=src, dst_ref=dst, send_sem=pair_send.at[which, chunk],
            recv_sem=pair_recv.at[which, chunk],
            device_id={"vblk": 1 - core}, device_id_type=MESH,
        )

    def loop(body):
        def step(chunk, carry):
            body(chunk)
            return carry

        lax.fori_loop(0, chunks, step, 0)

    @pl.when(has_next)
    def _():
        for index in range(LZ):
            link_copy(index).start()

    @pl.when(has_up)
    def _():
        link_copy(LZ).start()

    loop(lambda chunk: start_halo(0, chunk))

    @pl.when(has_prev)
    def _():
        for index in range(LZ):
            link_copy(index).wait_recv()

    @pl.when(has_down)
    def _():
        link_copy(LZ).wait_recv()

    for z in range(LZ):
        lanes = pl.ds(z * LAYER, LAYER)
        forward = [link_ref[mu, :, lanes] for mu in range(3)]
        below = link_z[...] if z == 0 else link_ref[2, :, pl.ds((z - 1) * LAYER, LAYER)]
        backward = [x_backward(forward[0]), y_backward(forward[1], link_y[z]), below]
        for side, table in enumerate((forward, backward)):
            for mu in range(3):
                for k in range(18):
                    spread[side, mu, k, z] = jnp.broadcast_to(
                        table[mu][k : k + 1], (8, LAYER)
                    )

    def hop(stage, chunk, finish):
        field = fields[stage]
        both = stage < 2
        own = pl.ds(pl.multiple_of(chunk * CHUNK, CHUNK), CHUNK)

        def shift(z, carry):
            for part_id in range(2):
                for colour in range(3):
                    layer = field[part_id, colour, z + 1, own, :]
                    moved[0, part_id, colour, z] = x_forward(layer)
                    moved[1, part_id, colour, z] = y_forward(
                        layer, y_after[stage, part_id, colour, z, own, :]
                    )
                    if both:
                        moved[2, part_id, colour, z] = x_backward(layer)
                        moved[3, part_id, colour, z] = y_backward(
                            layer, y_before[stage, part_id, colour, z, own, :]
                        )
            return carry

        lax.fori_loop(0, LZ, shift, 0)

        def take(ref, *at):
            return ref[at].reshape(CHUNK // 8, 8, 128)

        def add_hops(pairs, z, lanes):
            acc_re = [None] * 3
            acc_im = [None] * 3
            for mu, side in pairs:
                if mu == 2:
                    here = [
                        take(field, c // 3, c % 3, z + (0 if side else 2), own, lanes)
                        for c in range(6)
                    ]
                else:
                    here = [
                        take(moved, 2 * side + mu, c // 3, c % 3, z, slice(None), lanes)
                        for c in range(6)
                    ]
                for row in range(3):
                    for col in range(3):
                        k = row * 3 + col if side == 0 else col * 3 + row
                        link_re = spread[side, mu, k, z, :, lanes]
                        link_im = spread[side, mu, 9 + k, z, :, lanes]
                        re, im = here[col], here[3 + col]
                        if side == 0:
                            real = link_re * re - link_im * im
                            imag = link_re * im + link_im * re
                        else:
                            real = link_re * re + link_im * im
                            imag = link_re * im - link_im * re
                        if acc_re[row] is None:
                            acc_re[row], acc_im[row] = real, imag
                        else:
                            acc_re[row] = acc_re[row] + real
                            acc_im[row] = acc_im[row] + imag
            return acc_re, acc_im

        def tile(index, carry):
            z = index // (LAYER // 128)
            lanes = pl.ds(pl.multiple_of(lax.rem(index, LAYER // 128) * 128, 128), 128)
            sides = (0, 1) if both else (0,)
            pairs = [(mu, side) for mu in range(3) for side in sides]
            sums_of = add_hops(pairs, z, lanes)
            for row in range(3):
                for part_id in range(2):
                    finish(part_id, row, z, own, lanes, sums_of[part_id][row])
            return carry

        def edge_tile(index, carry):
            lanes = pl.ds(pl.multiple_of(index * 128, 128), 128)
            sums_of = add_hops([(2, 1)], 0, lanes)
            for row in range(3):
                for part_id in range(2):
                    there = merged(b_own, part_id, row, 0, own, lanes)
                    finish(part_id, row, 0, own, lanes, there + sums_of[part_id][row])
            return carry

        lax.fori_loop(0, LZ * LAYER // 128, tile, 0)
        if not both:
            lax.fori_loop(0, LAYER // 128, edge_tile, 0)

    def merged(ref, part_id, row, z, own, lanes):
        return ref[part_id, row, z, own, lanes].reshape(CHUNK // 8, 8, 128)

    def finish_first(part_id, row, z, own, lanes, value):
        center = merged(e_v, part_id, row, z + 1, own, lanes)
        done = (OWN * center - value) * (1.0 / half_width)
        e_first[part_id, row, z + 1, own, lanes] = done.reshape(CHUNK, 128)

    def finish_filtered(part_id, row, z, own, lanes, value):
        center = merged(e_first, part_id, row, z + 1, own, lanes)
        start = merged(e_v, part_id, row, z + 1, own, lanes)
        done = (OWN * center - value) * (2.0 / half_width) - start
        e_filt[part_id, row, z + 1, own, lanes] = done.reshape(CHUNK, 128)

    def finish_bonds(part_id, row, z, own, lanes, value):
        b_own[part_id, row, z, own, lanes] = value.reshape(CHUNK, 128)

    def do_first(chunk):
        await_halo(0, chunk)
        hop(0, chunk, finish_first)
        start_halo(1, chunk)

    def do_filtered(chunk):
        await_halo(1, chunk)
        hop(1, chunk, finish_filtered)
        pair_copy(0, chunk).start()
        start_halo(2, chunk)

    def do_bonds(chunk):
        await_halo(2, chunk)
        hop(2, chunk, finish_bonds)
        pair_copy(1, chunk).start()

    for c in range(2):

        @pl.when(core == c)
        def _(c=c):
            columns[...] = turn_ref[:, :, pl.ds(c * count, count)]

    loop(do_first)
    loop(do_filtered)
    loop(lambda chunk: pair_copy(0, chunk).wait_recv())

    def stacked(ref, colour, z):
        return halves(jnp.concatenate([ref[0, colour, z], ref[1, colour, z]], axis=0))

    lane_dims = ((1,), (1,))
    sums[...] = jnp.zeros_like(sums)
    turn = []
    for at in (core, 1 - core):
        real, imag = [
            columns[c, pl.ds(pl.multiple_of(at * count, 8), count), :] for c in range(2)
        ]
        left = jnp.concatenate(
            [jnp.concatenate([real, imag], 1), jnp.concatenate([-imag, real], 1)], 0
        )
        turn.append(halves(left))

    for colour in range(3):
        for z in range(LZ):
            mine = stacked(e_filt, colour, z + 1)
            other = stacked(f_other, colour, z)
            sums[0] += split_dot(mine, mine, lane_dims)
            sums[1] += split_dot(other, mine, lane_dims)
            turned = split_dot(turn[0], mine, ((0,), (0,)))
            turned = turned + split_dot(turn[1], other, ((0,), (0,)))
            for part_id in range(2):
                out_ref[part_id, colour, :, pl.ds(z * LAYER, LAYER)] = turned[
                    part_id * count : (part_id + 1) * count
                ]

    def inner(index):
        top = sums[index, pl.ds(0, count), :]
        low = sums[index, pl.ds(count, count), :]
        return (
            top[:, :count] + low[:, count:],
            top[:, count:] - low[:, :count],
        )

    sites = 3.0 * n * vec_ref.shape[3]
    spare = 128 - count
    full = -(-4 * count // 128)
    proj_blocks = []

    def pack(which, blocks):
        fill = jnp.zeros((count, full * spare - (4 - full) * count), jnp.float32)
        tail = jnp.concatenate(blocks[full:] + [fill], axis=1)
        for index in range(full):
            part[which, pl.ds(index * count, count), :] = jnp.concatenate(
                [blocks[index], tail[:, index * spare : (index + 1) * spare]], axis=1
            )
        left = part.shape[1] - full * count
        if left:
            part[which, pl.ds(full * count, left), :] = jnp.zeros((left, 128), jnp.float32)

    def unpack(which, ref):
        packed = [total[which, pl.ds(index * count, count), :] for index in range(full)]
        tail = jnp.concatenate([block[:, count:] for block in packed], axis=1)
        found = [block[:, :count] for block in packed]
        found += [tail[:, i * count : (i + 1) * count] for i in range(4 - full)]
        for side, at in ((0, core), (1, 1 - core)):
            for part_id in range(2):
                ref[part_id, pl.ds(pl.multiple_of(at * count, 8), count), :] = found[
                    2 * side + part_id
                ]

    def around(body):
        def step(d, carry):
            body(d)
            return carry

        lax.fori_loop(1, n, step, 0)

    def rows_of(owner):
        return pl.ds(pl.multiple_of(owner * rows, 8), rows)

    def part_copy(which, d):
        owner = lax.rem(me + d, n)
        return pltpu.make_async_remote_copy(
            src_ref=part.at[which, rows_of(owner)], dst_ref=slots.at[which, d],
            send_sem=part_send.at[which, d], recv_sem=part_recv.at[which, d],
            device_id={"slab": owner}, device_id_type=MESH,
        )

    def total_copy(which, d, source):
        return pltpu.make_async_remote_copy(
            src_ref=total.at[which, rows_of(source)], dst_ref=total.at[which, rows_of(source)],
            send_sem=total_send.at[which, d], recv_sem=total_recv.at[which, d],
            device_id={"slab": lax.rem(me + d, n)}, device_id_type=MESH,
        )

    def gather_sums(which):
        around(lambda d: part_copy(which, d).wait_recv())
        total[which, rows_of(me), :] = lax.fori_loop(
            1, n, lambda d, running: running + slots[which, d], part[which, rows_of(me), :]
        )
        around(lambda d: total_copy(which, d, me).start())

    result = pltpu.make_async_copy(out_ref, result_ref, out_sem)
    result.start()
    pack(0, [value * (1.0 / sites) for side in range(2) for value in inner(side)])
    around(lambda d: part_copy(0, d).start())
    loop(do_bonds)
    gather_sums(0)

    for colour in range(3):
        for z in range(LZ):
            mine = stacked(e_filt, colour, z + 1)
            other = stacked(f_other, colour, z)
            bond = stacked(b_own, colour, z)
            sums[2] += split_dot(mine, bond, lane_dims) + split_dot(bond, mine, lane_dims)
            sums[3] += split_dot(other, bond, lane_dims)

    loop(lambda chunk: pair_copy(1, chunk).wait_recv())

    for colour in range(3):
        for z in range(LZ):
            mine = stacked(e_filt, colour, z + 1)
            bond_other = stacked(b_other, colour, z)
            sums[3] += split_dot(bond_other, mine, lane_dims)

    for side in range(2):
        grams, bonds = inner(side), inner(2 + side)
        for part_id in range(2):
            projected = (OWN * grams[part_id] - bonds[part_id]) * (1.0 / half_width)
            proj_blocks.append(projected * (1.0 / sites))
    pack(1, proj_blocks)
    around(lambda d: part_copy(1, d).start())
    around(lambda d: total_copy(0, d, lax.rem(me + n - d, n)).wait_recv())
    unpack(0, gram_ref)
    gather_sums(1)
    around(lambda d: total_copy(1, d, lax.rem(me + n - d, n)).wait_recv())
    unpack(1, proj_ref)

    def end_sends(chunk):
        for stage in range(3):
            for kind in kinds[stage]:
                pl.when(sends[kind])(
                    lambda stage=stage, kind=kind: halo(stage, kind, chunk).wait_send()
                )
        for which in range(2):
            pair_copy(which, chunk).wait_send()

    loop(end_sends)

    @pl.when(has_next)
    def _():
        for index in range(LZ):
            link_copy(index).wait_send()

    @pl.when(has_up)
    def _():
        link_copy(LZ).wait_send()

    for which in range(2):
        around(lambda d: part_copy(which, d).wait_send())
        around(lambda d: total_copy(which, d, me).wait_send())
    result.wait()


def per_device(n, vectors, links, rotation):
    count, local_sites = vectors.shape[2], vectors.shape[3]
    chunks = count // CHUNK
    rows = 8 * -(-(-(-4 * count // 128) * count) // (8 * n))
    all_rows = n * rows
    f32 = jnp.float32
    halo_shape = (2, 3, LZ + 2, count, LAYER)
    block = (2, 3, LZ, count, LAYER)
    vmem = pl.BlockSpec(memory_space=pltpu.VMEM)
    return pl.pallas_call(
        functools.partial(kernel, n, rows),
        out_shape=(
            jax.ShapeDtypeStruct(vectors.shape, f32),
            jax.ShapeDtypeStruct((2, 2 * count, count), f32),
            jax.ShapeDtypeStruct((2, 2 * count, count), f32),
        ),
        in_specs=[pl.BlockSpec(memory_space=pl.ANY), vmem, vmem],
        out_specs=(pl.BlockSpec(memory_space=pl.ANY), vmem, vmem),
        scratch_shapes=[
            pltpu.VMEM(halo_shape, f32),
            pltpu.VMEM(halo_shape, f32),
            pltpu.VMEM(halo_shape, f32),
            pltpu.VMEM((2, 2, 3, LZ, count, 128), f32),
            pltpu.VMEM((3, 2, 3, LZ, count, 128), f32),
            pltpu.VMEM((LZ, 18, 128), f32),
            pltpu.VMEM((18, LAYER), f32),
            pltpu.VMEM((2, 3, 18, LZ, 8, LAYER), f32),
            pltpu.VMEM((4, 2, 3, LZ, CHUNK, LAYER), f32),
            pltpu.VMEM(block, f32),
            pltpu.VMEM(block, f32),
            pltpu.VMEM(block, f32),
            pltpu.VMEM((4, 2 * count, 2 * count), f32),
            pltpu.VMEM((2, all_rows, 128), f32),
            pltpu.VMEM((2, n, rows, 128), f32),
            pltpu.VMEM((2, all_rows, 128), f32),
            pltpu.SemaphoreType.DMA((LZ,)),
            pltpu.SemaphoreType.DMA((3, 6, chunks)),
            pltpu.SemaphoreType.DMA((3, 6, chunks)),
            pltpu.SemaphoreType.DMA((LZ + 1,)),
            pltpu.SemaphoreType.DMA((LZ + 1,)),
            pltpu.SemaphoreType.DMA((2, chunks)),
            pltpu.SemaphoreType.DMA((2, chunks)),
            pltpu.SemaphoreType.DMA((2, n)),
            pltpu.SemaphoreType.DMA((2, n)),
            pltpu.SemaphoreType.DMA((2, n)),
            pltpu.SemaphoreType.DMA((2, n)),
            pltpu.VMEM((3, 18, local_sites), f32),
            pltpu.VMEM((2, 2 * count, count), f32),
            pltpu.VMEM(vectors.shape, f32),
            pltpu.SemaphoreType.DMA,
        ],
        compiler_params=pltpu.CompilerParams(
            collective_id=0, has_side_effects=True, vmem_limit_bytes=56 * 1024 * 1024
        ),
    )(vectors, jnp.transpose(links, (1, 2, 0, 3)), rotation)


def solution(mesh):
    in_specs = (
        P(None, None, "vblk", ("parts", "slab")),
        P(None, None, None, ("parts", "slab")),
        P(),
    )
    out_specs = (
        P(None, None, "vblk", ("parts", "slab")),
        P("parts", None, "vblk"),
        P("parts", None, "vblk"),
    )
    return jax.shard_map(
        functools.partial(per_device, mesh.shape["slab"]),
        mesh=mesh, in_specs=in_specs, out_specs=out_specs, check_vma=False,
    )
```
